32 devices in a mesh: tile: 8 (over y, x, core), mode: 4 (over z).
Axes of the slice: x: 2, y: 2, z: 4, core: 2. Of those that a mesh axis runs over, the one named last changes fastest.
Arguments:
- mode_shapes: bfloat16 [64, 64, 2048], P('mode', 'tile'), may hold values from -6 to 6
- stiffness: float32 [64, 2048], P('tile'), may hold values from 0.5 to 4
- node_slot: int32 [64, 2048], P('tile'), may hold values from 0 to 63, as said below
- slot_zone: int32 [8, 8, 8], replicated, may hold values from 0 to 63, as said below
Outputs:
- energy: float32 [512, 64, 64], P('tile', 'mode')
The draws below stay inside these ranges and needn't reach their ends.
Inputs may be any that keep to these rules, and one draw needn't show every extreme that they name: `slot_zone`: for each tile and owner, the 8 zone numbers are distinct. `node_slot`: slots that no node of a tile names carry no zone's nodes.
All inputs are finite; a program needn't handle non-finite values.
Results may differ from the reference program's by a relative error of at most 0.00099.
Values may be sent and summed in bfloat16 or wider, within the bound.
A program may use at most 64 MiB of HBM per device.

```python
import math
import jax
import jax.numpy as jnp
from jax import lax

MODES = 64
ZONES = 512
CAP = 8
RX = 8
NY = 2048
NX = 64
ZONE_DEV = 64
SLOTS = 64
N_TILE = 8


def draw_node_slot(key, part):
    key_counts = jax.random.fold_in(key, 11)
    key_owner = jax.random.fold_in(key, 12)
    key_entry = jax.random.fold_in(key, 13)
    counts = jax.random.randint(key_counts, (N_TILE, N_TILE), 1, CAP + 1)
    counts = counts.at[:, N_TILE - 1].set(CAP)
    owner_tile = jax.random.randint(key_owner, (NX, NY), 0, N_TILE)
    entry_bits = jax.random.randint(key_entry, (NX, NY), 0, 1 << 20)
    tile_of = jnp.arange(NX) // RX
    live_count = counts[tile_of[:, None], owner_tile]
    slot_ids = owner_tile * CAP + entry_bits % live_count
    row_place = jnp.arange(NX)[:, None] % RX
    column_place = jnp.arange(NY)[None, :]
    slot_ids = jnp.where((row_place == RX - 1) & (column_place == NY - 1), SLOTS - 1, slot_ids)
    slot_ids = jnp.where((row_place == 0) & (column_place == 0), 0, slot_ids)
    return slot_ids.astype(jnp.int32)


def draw_slot_zone(key, part):
    key_scores = jax.random.fold_in(key, 21)
    scores = jax.random.randint(key_scores, (N_TILE, N_TILE, ZONE_DEV), 0, 1 << 16) * ZONE_DEV + jnp.arange(ZONE_DEV)
    ordering = jnp.argsort(scores, axis=-1, stable=True)
    return ordering[:, :, :CAP].astype(jnp.int32)


def block_levels(key, dims, shards, low, largest):
    level = 1.0
    for position, blocks in shards:
        heights = jax.random.uniform(jax.random.fold_in(jax.random.fold_in(key, 6), position), (blocks,), jnp.float32, low / len(shards), largest / len(shards))
        level = level * jnp.repeat(jnp.exp(heights), dims[position] // blocks).reshape((-1,) + (1,) * (len(dims) - 1 - position))
    return level


def scatter_about(rng, dims, deviation, reach, split=(), held_as=jnp.bfloat16):
    drawn = deviation * jax.random.normal(rng, dims, jnp.float32)
    if split:
        drawn = drawn * block_levels(rng, dims, split, -0.22, 0.18)
    return jnp.clip(drawn, -reach, reach).astype(held_as)


def setup_inputs(seed: int = 0) -> dict:
    key_list = jax.random.split(jax.random.key(seed), 5)
    return {
        "mode_shapes": scatter_about(key_list[0], (MODES, NX, NY), 1.0, 6.0, ((0, 4), (1, 8))),
        "stiffness": jnp.clip(jnp.exp(math.log(4.0) - 2.0794415 * jax.random.uniform(key_list[1], (NX, NY), jnp.float32) ** block_levels(key_list[1], (NX, NY), ((0, 8),), -0.2, 0.2)), 0.5, 4.0),
        "node_slot": draw_node_slot(jax.random.fold_in(key_list[4], 71), 0),
        "slot_zone": draw_slot_zone(jax.random.fold_in(key_list[4], 71), 0),
    }


POISSON = 0.3
SHEAR = 2.0 * (1.0 - POISSON)

def curvatures(shapes_framed):
    framed = jnp.pad(shapes_framed, ((0, 0), (0, 0), (1, 1)))
    centre = framed[:, 1:-1, 1:-1]
    along_x = framed[:, 2:, 1:-1] - 2.0 * centre + framed[:, :-2, 1:-1]
    along_y = framed[:, 1:-1, 2:] - 2.0 * centre + framed[:, 1:-1, :-2]
    twist_xy = 0.25 * (framed[:, 2:, 2:] - framed[:, 2:, :-2] - framed[:, :-2, 2:] + framed[:, :-2, :-2])
    return jnp.stack([along_x, along_y, twist_xy]).astype(jnp.bfloat16)

def left_factor(bending, stiffness):
    along_x, along_y, twist_xy = (bending[0], bending[1], bending[2])
    return jnp.stack([stiffness * (along_x + POISSON * along_y), stiffness * (along_y + POISSON * along_x), stiffness * (SHEAR * twist_xy)])

def reference(mode_shapes, stiffness, node_slot, slot_zone):
    framed = jnp.pad(mode_shapes.astype(jnp.float32), ((0, 0), (1, 1), (0, 0)))
    bending = lax.optimization_barrier(curvatures(framed)).astype(jnp.float32)
    weighted = left_factor(bending, stiffness)
    totals = 0.5 * lax.optimization_barrier(jnp.sum(weighted * bending, axis=(0, 2, 3)))
    left_round = lax.optimization_barrier(weighted.astype(jnp.bfloat16)).astype(jnp.float32)
    node_total = NX * NY
    left_flat = left_round.reshape(3, MODES, node_total)
    right_flat = bending.reshape(3, MODES, node_total)
    tile_of = jnp.arange(NX, dtype=jnp.int32) // RX
    owner_tile = node_slot // CAP
    within = node_slot % CAP
    zone_ids = (owner_tile * ZONE_DEV + slot_zone[tile_of[:, None], owner_tile, within]).reshape(node_total)
    block_nodes = math.gcd(node_total, 2048)

    def one_block(number, running):
        first_node = number * block_nodes
        left_block = lax.dynamic_slice_in_dim(left_flat, first_node, block_nodes, 2)
        right_block = lax.dynamic_slice_in_dim(right_flat, first_node, block_nodes, 2)
        zone_block = lax.dynamic_slice_in_dim(zone_ids, first_node, block_nodes, 0)
        outer_terms = jnp.einsum('cin,cjn->nij', left_block, right_block, precision=lax.Precision.HIGHEST)
        return running + jax.ops.segment_sum(outer_terms, zone_block, num_segments=ZONES)
    summed = lax.fori_loop(0, node_total // block_nodes, one_block, jnp.zeros((ZONES, MODES, MODES), jnp.float32))
    return ZONES * (0.5 * summed) / jnp.sqrt(totals[:, None] * totals[None, :])
```

```python
import functools

import jax
import jax.numpy as jnp
from jax import lax
from jax.experimental import pallas as pl
from jax.experimental.pallas import tpu as pltpu
from jax.sharding import PartitionSpec as P

ZONES = 512
POISSON = 0.3
SHEAR = 2.0 * (1.0 - POISSON)
LANES = 128


def bend_row(frame_ref, row, first_col, last_col):
    up = frame_ref[row].astype(jnp.float32)
    mid = frame_ref[row + 1].astype(jnp.float32)
    down = frame_ref[row + 2].astype(jnp.float32)
    width = mid.shape[1]

    def before(cells):
        return jnp.where(first_col, 0.0, pltpu.roll(cells, 1, 1))

    def after(cells):
        return jnp.where(last_col, 0.0, pltpu.roll(cells, width - 1, 1))

    along_x = down - 2.0 * mid + up
    along_y = after(mid) - 2.0 * mid + before(mid)
    slope = down - up
    twist = 0.25 * (after(slope) - before(slope))
    return [c.astype(jnp.bfloat16) for c in (along_x, along_y, twist)]


def pair_kernel(owners, entries, a_ref, b_ref, stiff_ref, slot_ref, acc_ref, sums_ref, left_s, right_s):
    rows = stiff_ref.shape[0]
    panel, width = a_ref.shape[1:]
    column = lax.broadcasted_iota(jnp.int32, (panel, width), 1)
    first_col = column == 0
    last_col = column == width - 1
    acc_ref[...] = jnp.zeros_like(acc_ref)
    sums_ref[...] = jnp.zeros_like(sums_ref)

    def one_row(row, carry):
        stiff = stiff_ref[row]
        slot = slot_ref[row]
        owner = slot // entries
        entry = slot - owner * entries
        owner_b = jnp.broadcast_to(owner, (panel, width))
        entry_b = jnp.broadcast_to(entry, (panel, width))
        lefts, rights = [], []
        for number, ref in enumerate((a_ref, b_ref)):
            bend = bend_row(ref, row, first_col, last_col)
            bx, by, bt = [c.astype(jnp.float32) for c in bend]
            lx = stiff * (bx + POISSON * by)
            ly = stiff * (by + POISSON * bx)
            lt = stiff * (SHEAR * bt)
            if number == 0:
                inside = jnp.sum(lx * bx + ly * by + lt * bt, axis=1, keepdims=True)
                sums_ref[...] += jnp.broadcast_to(inside, sums_ref.shape)
            rights.append(bend)
            lefts.append([c.astype(jnp.bfloat16) for c in (lx, ly, lt)])
        for k in range(owners):
            mask = (owner_b == k).astype(jnp.float32).astype(jnp.bfloat16)
            for c in range(3):
                for n in range(2):
                    left_s[c, pl.ds((n * owners + k) * panel, panel), :] = lefts[n][c] * mask
        for k in range(entries):
            mask = (entry_b == k).astype(jnp.float32).astype(jnp.bfloat16)
            for c in range(3):
                for n in range(2):
                    right_s[c, pl.ds((n * entries + k) * panel, panel), :] = rights[n][c] * mask
        for c in range(3):
            acc_ref[...] += lax.dot_general(
                left_s[c], right_s[c], (((1,), (1,)), ((), ())), preferred_element_type=jnp.float32
            )
        return carry

    lax.fori_loop(0, rows, one_row, 0)


def pair_sums(own, other, stiff, slot, owners, entries):
    rows = stiff.shape[0]
    panel, width = own.shape[1:]
    tall, wide = 2 * owners * panel, 2 * entries * panel
    whole = pl.BlockSpec(memory_space=pltpu.VMEM)
    return pl.pallas_call(
        functools.partial(pair_kernel, owners, entries),
        out_shape=(
            jax.ShapeDtypeStruct((tall, wide), jnp.float32),
            jax.ShapeDtypeStruct((panel, LANES), jnp.float32),
        ),
        in_specs=[whole] * 4,
        out_specs=(whole, whole),
        scratch_shapes=[
            pltpu.VMEM((3, tall, width), jnp.bfloat16),
            pltpu.VMEM((3, wide, width), jnp.bfloat16),
        ],
        compiler_params=pltpu.CompilerParams(vmem_limit_bytes=48 << 20),
        cost_estimate=pl.CostEstimate(
            flops=2 * 3 * tall * wide * rows * width,
            bytes_accessed=4 * rows * panel * width * 2,
            transcendentals=0,
        ),
    )(own, other, stiff.reshape(rows, 1, width), slot.reshape(rows, 1, width))


def zone_kernel(place_ref, source_ref, blocks_ref, scale_ref, out_ref):
    panels, tiles, panel, _ = blocks_ref.shape
    entries = source_ref.shape[1]
    me = place_ref[0]
    out_ref[...] = jnp.zeros_like(out_ref)
    scale = scale_ref[...]

    def one_tile(tile, carry):
        got = [blocks_ref[lax.rem(g - me + panels, panels), tile] for g in range(panels)]
        for k in range(entries):
            row = jnp.concatenate([b[:, k * panel : (k + 1) * panel] for b in got], axis=1)
            zone = source_ref[tile, k]
            out_ref[zone] += row * scale
        return carry

    lax.fori_loop(0, tiles, one_tile, 0)


def per_device(mode_shapes, stiffness, node_slot, slot_zone):
    panel, rows, width = mode_shapes.shape
    tiles = lax.axis_size("tile")
    panels = lax.axis_size("mode")
    modes = panel * panels
    entries = slot_zone.shape[2]
    owned = ZONES // tiles
    me = lax.axis_index("mode")
    tile = lax.axis_index("tile")
    half = panels // 2

    own = mode_shapes.transpose(1, 0, 2)
    below = lax.ppermute(own[-1:], "tile", [(i, i + 1) for i in range(tiles - 1)])
    above = lax.ppermute(own[:1], "tile", [(i + 1, i) for i in range(tiles - 1)])
    frame = jnp.concatenate([below, own, above], axis=0)

    part = width // 2 + LANES
    shift = width // 2 - LANES
    mine_start = jnp.where(me < half, 0, shift)
    their_start = jnp.where(me < half, shift, 0)
    sent_half = lax.dynamic_slice_in_dim(frame, their_start, part, 2)
    others = [
        lax.ppermute(frame, "mode", [(i, (i - d) % panels) for i in range(panels)]) for d in range(1, half)
    ]
    other_half = lax.ppermute(sent_half, "mode", [(i, (i - half) % panels) for i in range(panels)])

    blocks = [None] * panels
    for d in range(1, half):
        acc, sums = pair_sums(frame, others[d - 1], stiffness, node_slot, tiles, entries)
        if d == 1:
            own_sums = sums[:, 0]
            blocks[0] = acc[: tiles * panel, : entries * panel]
        blocks[d] = acc[: tiles * panel, entries * panel :]
        blocks[panels - d] = lax.ppermute(
            acc[tiles * panel :, : entries * panel], "mode", [(i, (i + d) % panels) for i in range(panels)]
        )
    placed = lax.dynamic_update_slice_in_dim(jnp.zeros((modes,), jnp.float32), own_sums, me * panel, 0)
    totals = 0.5 * lax.psum(placed, ("tile", "mode"))

    own_half = lax.dynamic_slice_in_dim(frame, mine_start, part, 2)
    stiff_half = lax.dynamic_slice_in_dim(stiffness, mine_start, part, 1)
    slot_half = lax.dynamic_slice_in_dim(node_slot, mine_start, part, 1)
    column = jnp.arange(part)[None, :]
    inside = jnp.where(me < half, column < width // 2, column >= LANES)
    slot_half = jnp.where(inside, slot_half, tiles * entries)
    acc, _ = pair_sums(own_half, other_half, stiff_half, slot_half, tiles, entries)
    returned = lax.ppermute(
        acc[tiles * panel :, : entries * panel], "mode", [(i, (i + half) % panels) for i in range(panels)]
    )
    blocks[half] = acc[: tiles * panel, entries * panel :] + returned

    stacked = jnp.stack(blocks).reshape(panels, tiles, panel, entries * panel)
    arrived = lax.all_to_all(stacked, "tile", split_axis=1, concat_axis=1, tiled=True)
    source = lax.dynamic_index_in_dim(slot_zone, tile, 1, keepdims=False)
    mine = lax.dynamic_slice_in_dim(totals, me * panel, panel, 0)
    scale = (0.5 * ZONES) / jnp.sqrt(mine[:, None] * totals[None, :])
    return pl.pallas_call(
        zone_kernel,
        out_shape=jax.ShapeDtypeStruct((owned, panel, modes), jnp.float32),
        in_specs=[
            pl.BlockSpec(memory_space=pltpu.SMEM),
            pl.BlockSpec(memory_space=pltpu.SMEM),
            pl.BlockSpec(memory_space=pltpu.VMEM),
            pl.BlockSpec(memory_space=pltpu.VMEM),
        ],
        out_specs=pl.BlockSpec(memory_space=pltpu.VMEM),
    )(me.reshape(1), source, arrived, scale)


def solution(mesh):
    placed = (P("mode", "tile", None), P("tile", None), P("tile", None), P())
    return jax.shard_map(
        per_device, mesh=mesh, in_specs=placed, out_specs=P("tile", "mode", None), check_vma=False
    )
```

```python
import functools

import jax
import jax.numpy as jnp
from jax import lax
from jax.experimental import pallas as pl
from jax.experimental.pallas import tpu as pltpu
from jax.sharding import PartitionSpec as P

ZONES = 512
POISSON = 0.3
SHEAR = 2.0 * (1.0 - POISSON)
LANES = 128


def bend_row(up, mid, down, first_col, last_col):
    up = up.astype(jnp.float32)
    mid = mid.astype(jnp.float32)
    down = down.astype(jnp.float32)
    width = mid.shape[1]

    def before(cells):
        return jnp.where(first_col, 0.0, pltpu.roll(cells, 1, 1))

    def after(cells):
        return jnp.where(last_col, 0.0, pltpu.roll(cells, width - 1, 1))

    along_x = down - 2.0 * mid + up
    along_y = after(mid) - 2.0 * mid + before(mid)
    slope = down - up
    twist = 0.25 * (after(slope) - before(slope))
    return [c.astype(jnp.bfloat16) for c in (along_x, along_y, twist)]


def pair_kernel(
    sizes, own_ref, stiff_ref, slot_ref, out_ref, total_ref,
    frames, half_frame, left_s, right_s, acc, sums, results, returned, arrived, tile_sums, mode_sums,
    halo_send, halo_recv, row_send, row_recv, back_send, back_recv, block_send, block_recv,
    tsum_send, tsum_recv, msum_send, msum_recv,
):
    tiles, panels, entries = sizes
    rows, panel, width = own_ref.shape
    half = panels // 2
    part = half_frame.shape[2]
    shift = width - part
    tall, wide = tiles * panel, entries * panel
    tile = lax.axis_index("tile")
    me = lax.axis_index("mode")

    def tile_peer(step):
        return lax.rem(tile + step, tiles)

    def mode_peer(step):
        return lax.rem(me + step, panels)

    def to(src, dst, send, recv, at_tile, at_mode):
        return pltpu.make_async_remote_copy(
            src_ref=src, dst_ref=dst, send_sem=send, recv_sem=recv,
            device_id=(at_tile, at_mode), device_id_type=pl.DeviceIdType.MESH,
        )

    barrier = pltpu.get_barrier_semaphore()
    for step in range(1, panels):
        pl.semaphore_signal(barrier, inc=1, device_id=(tile, mode_peer(step)), device_id_type=pl.DeviceIdType.MESH)

    def greet(step, carry):
        pl.semaphore_signal(barrier, inc=1, device_id=(tile_peer(step), me), device_id_type=pl.DeviceIdType.MESH)
        return carry

    lax.fori_loop(1, tiles, greet, 0)

    first_tile, last_tile = tile == 0, tile == tiles - 1

    @pl.when(first_tile)
    def _():
        for d in range(half):
            frames[d, 0] = jnp.zeros((panel, width), jnp.bfloat16)
        half_frame[0] = jnp.zeros((panel, part), jnp.bfloat16)

    @pl.when(last_tile)
    def _():
        for d in range(half):
            frames[d, rows + 1] = jnp.zeros((panel, width), jnp.bfloat16)
        half_frame[rows + 1] = jnp.zeros((panel, part), jnp.bfloat16)

    pl.semaphore_wait(barrier, panels - 1 + tiles - 1)

    their_start = pl.multiple_of(jnp.where(me < half, shift, 0), LANES)
    mine_start = pl.multiple_of(jnp.where(me < half, 0, shift), LANES)

    def row_copy(d, row):
        if d == half:
            src, dst = own_ref.at[row, :, pl.ds(their_start, part)], half_frame.at[row + 1]
        else:
            src, dst = own_ref.at[row], frames.at[d, row + 1]
        return to(src, dst, row_send.at[d, row], row_recv.at[d, row], tile, mode_peer(panels - d))

    def edge_copies(d):
        frame = half_frame if d == half else frames.at[d]
        top = own_ref.at[0] if d == 0 else frame.at[1]
        bottom = own_ref.at[rows - 1] if d == 0 else frame.at[rows]
        upward = to(top, frame.at[rows + 1], halo_send.at[d, 0], halo_recv.at[d, 0], jnp.maximum(tile - 1, 0), me)
        downward = to(
            bottom, frame.at[0], halo_send.at[d, 1], halo_recv.at[d, 1], jnp.minimum(tile + 1, tiles - 1), me
        )
        return upward, downward

    def start_edges(d):
        upward, downward = edge_copies(d)
        pl.when(jnp.logical_not(first_tile))(upward.start)
        pl.when(jnp.logical_not(last_tile))(downward.start)

    def await_edges(d):
        upward, downward = edge_copies(d)
        pl.when(jnp.logical_not(last_tile))(upward.wait_recv)
        pl.when(jnp.logical_not(first_tile))(downward.wait_recv)

    def finish_edges(d):
        upward, downward = edge_copies(d)
        pl.when(jnp.logical_not(first_tile))(upward.wait_send)
        pl.when(jnp.logical_not(last_tile))(downward.wait_send)

    start_edges(0)
    for d in range(1, half + 1):
        row_copy(d, 0).start()
        row_copy(d, rows - 1).start()
    for d in range(1, half + 1):
        for row in range(1, rows - 1):
            row_copy(d, row).start()
    for row in range(rows):
        frames[0, row + 1] = own_ref[row]

    sums[...] = jnp.zeros_like(sums)

    def block_copy(block, step):
        peer = tile_peer(step)
        return to(
            results.at[block, peer], arrived.at[block, tile],
            block_send.at[block, step], block_recv.at[block, step], peer, me,
        )

    def start_blocks(block):
        def go(step, carry):
            block_copy(block, step).start()
            return carry

        lax.fori_loop(1, tiles, go, 0)
        arrived[block, tile] = results[block, tile]

    def back_copy(d):
        block = results.at[panels + d]
        return to(block, returned.at[d], back_send.at[d], back_recv.at[d], tile, mode_peer(d))

    def tsum_copy(step):
        return to(sums, tile_sums.at[tile], tsum_send.at[step], tsum_recv.at[step], tile_peer(step), me)

    def keep(block, values):
        results[block] = values.reshape(tiles, panel, wide)

    for d in range(1, half + 1):
        split = d == half
        span = part if split else width
        column = lax.broadcasted_iota(jnp.int32, (panel, span), 1)
        first_col, last_col = column == 0, column == span - 1
        if split:
            inside = jnp.where(me < half, (column < width // 2).astype(jnp.int32), (column >= LANES).astype(jnp.int32))
        row_copy(d, 0).wait_recv()
        row_copy(d, rows - 1).wait_recv()
        start_edges(d)
        row_copy(d, 1).wait_recv()
        acc[...] = jnp.zeros_like(acc)

        def one_row(k, carry):
            row = lax.rem(k + 1, rows)

            @pl.when(k < rows - 3)
            def _():
                row_copy(d, k + 2).wait_recv()

            @pl.when(k == rows - 2)
            def _():
                if d == 1:
                    await_edges(0)
                await_edges(d)

            if split:
                here = pl.ds(mine_start, part)
                stiff, slot = stiff_ref[row, :, here], slot_ref[row, :, here]
                mine = [frames[0, row + i, :, here] for i in range(3)]
                theirs = [half_frame[row + i] for i in range(3)]
            else:
                stiff, slot = stiff_ref[row], slot_ref[row]
                mine = [frames[0, row + i] for i in range(3)]
                theirs = [frames[d, row + i] for i in range(3)]
            owner = slot // entries
            entry = slot - owner * entries
            owner_b = jnp.broadcast_to(owner, (panel, span))
            entry_b = jnp.broadcast_to(entry, (panel, span))
            if split:
                owner_b = jnp.where(inside == 1, owner_b, tiles)
            lefts, rights = [], []
            for number, taken in enumerate((mine, theirs)):
                bend = bend_row(*taken, first_col, last_col)
                bx, by, bt = [c.astype(jnp.float32) for c in bend]
                lx = stiff * (bx + POISSON * by)
                ly = stiff * (by + POISSON * bx)
                lt = stiff * (SHEAR * bt)
                if number == 0 and d == 1:
                    row_sum = jnp.sum(lx * bx + ly * by + lt * bt, axis=1, keepdims=True)
                    sums[...] += jnp.broadcast_to(row_sum, sums.shape)
                rights.append(bend)
                lefts.append([c.astype(jnp.bfloat16) for c in (lx, ly, lt)])
            for k in range(tiles):
                mask = (owner_b == k).astype(jnp.float32).astype(jnp.bfloat16)
                for c in range(3):
                    for n in range(2):
                        left_s[c, pl.ds((n * tiles + k) * panel, panel), pl.ds(0, span)] = lefts[n][c] * mask
            for k in range(entries):
                mask = (entry_b == k).astype(jnp.float32).astype(jnp.bfloat16)
                for c in range(3):
                    for n in range(2):
                        right_s[c, pl.ds((n * entries + k) * panel, panel), pl.ds(0, span)] = rights[n][c] * mask
            for c in range(3):
                acc[...] += lax.dot_general(
                    left_s[c, :, pl.ds(0, span)], right_s[c, :, pl.ds(0, span)],
                    (((1,), (1,)), ((), ())), preferred_element_type=jnp.float32,
                )
            return carry

        lax.fori_loop(0, rows, one_row, 0)
        keep(panels + d, acc[pl.ds(tall, tall), pl.ds(0, wide)])
        back_copy(d).start()
        if d == 1:

            def send_sum(step, carry):
                tsum_copy(step).start()
                return carry

            lax.fori_loop(1, tiles, send_sum, 0)
            tile_sums[tile] = sums[...]
            keep(0, acc[pl.ds(0, tall), pl.ds(0, wide)])
            start_blocks(0)
        values = acc[pl.ds(0, tall), pl.ds(wide, wide)]
        if split:
            def take_sum(step, carry):
                tsum_copy(step).wait()
                return carry

            lax.fori_loop(1, tiles, take_sum, 0)
            mode_sums[me] = jnp.sum(tile_sums[...], axis=0)
            msums = [
                to(mode_sums.at[me], mode_sums.at[me], msum_send.at[step], msum_recv.at[step], tile, mode_peer(step))
                for step in range(1, panels)
            ]
            for copy in msums:
                copy.start()
            for e in range(1, half):
                back_copy(e).wait()
                results[panels - e] = returned[e]
                start_blocks(panels - e)
            back_copy(d).wait()
            keep(half, values)
            results[half] += returned[half]
            start_blocks(half)
        else:
            keep(d, values)
            start_blocks(d)

    for d in range(half + 1):
        finish_edges(d)
    for d in range(1, half + 1):
        for row in range(rows):
            row_copy(d, row).wait_send()
    for copy in msums:
        copy.wait()

    for block in range(panels):
        def take(step, carry):
            block_copy(block, step).wait()
            return carry

        lax.fori_loop(1, tiles, take, 0)
    out_ref[...] = arrived[...]
    total_ref[...] = mode_sums[...]


def pair_sums(own, stiff, slot, tiles, panels, entries):
    rows, panel, width = own.shape
    half = panels // 2
    part = width // 2 + LANES
    tall, wide = 2 * tiles * panel, 2 * entries * panel
    whole = pl.BlockSpec(memory_space=pltpu.VMEM)
    blocks = (panels, tiles, panel, entries * panel)
    dma = pltpu.SemaphoreType.DMA
    f32, bf16 = jnp.float32, jnp.bfloat16
    return pl.pallas_call(
        functools.partial(pair_kernel, (tiles, panels, entries)),
        out_shape=(
            jax.ShapeDtypeStruct(blocks, f32),
            jax.ShapeDtypeStruct((panels, panel, LANES), f32),
        ),
        in_specs=[whole] * 3,
        out_specs=(whole, whole),
        scratch_shapes=[
            pltpu.VMEM((half, rows + 2, panel, width), bf16),
            pltpu.VMEM((rows + 2, panel, part), bf16),
            pltpu.VMEM((3, tall, width), bf16),
            pltpu.VMEM((3, wide, width), bf16),
            pltpu.VMEM((tall, wide), f32),
            pltpu.VMEM((panel, LANES), f32),
            pltpu.VMEM((panels + half + 1,) + blocks[1:], f32),
            pltpu.VMEM((half + 1,) + blocks[1:], f32),
            pltpu.VMEM(blocks, f32),
            pltpu.VMEM((tiles, panel, LANES), f32),
            pltpu.VMEM((panels, panel, LANES), f32),
            dma((half + 1, 2)), dma((half + 1, 2)),
            dma((half + 1, rows)), dma((half + 1, rows)),
            dma((half + 1,)), dma((half + 1,)),
            dma((panels, tiles)), dma((panels, tiles)),
            dma((tiles,)), dma((tiles,)),
            dma((panels,)), dma((panels,)),
        ],
        compiler_params=pltpu.CompilerParams(
            vmem_limit_bytes=48 << 20, collective_id=0, has_side_effects=True
        ),
        cost_estimate=pl.CostEstimate(
            flops=6 * tall * wide * rows * width * half, bytes_accessed=2 * own.size * 2, transcendentals=0
        ),
    )(own, stiff.reshape(rows, 1, width), slot.reshape(rows, 1, width))


def zone_kernel(place_ref, source_ref, blocks_ref, scale_ref, out_ref):
    panels, tiles, panel, _ = blocks_ref.shape
    entries = source_ref.shape[1]
    me = place_ref[0]
    out_ref[...] = jnp.zeros_like(out_ref)
    scale = scale_ref[...]

    def one_tile(tile, carry):
        got = [blocks_ref[lax.rem(g - me + panels, panels), tile] for g in range(panels)]
        for k in range(entries):
            row = jnp.concatenate([b[:, k * panel : (k + 1) * panel] for b in got], axis=1)
            zone = source_ref[tile, k]
            out_ref[zone] += row * scale
        return carry

    lax.fori_loop(0, tiles, one_tile, 0)


def per_device(mode_shapes, stiffness, node_slot, slot_zone):
    panel = mode_shapes.shape[0]
    tiles = lax.axis_size("tile")
    panels = lax.axis_size("mode")
    modes = panel * panels
    entries = slot_zone.shape[2]
    owned = ZONES // tiles
    me = lax.axis_index("mode")
    tile = lax.axis_index("tile")

    own = mode_shapes.transpose(1, 0, 2)
    arrived, sums = pair_sums(own, stiffness, node_slot, tiles, panels, entries)
    totals = 0.5 * sums[:, :, 0].reshape(modes)
    source = lax.dynamic_index_in_dim(slot_zone, tile, 1, keepdims=False)
    mine = lax.dynamic_slice_in_dim(totals, me * panel, panel, 0)
    scale = (0.5 * ZONES) / jnp.sqrt(mine[:, None] * totals[None, :])
    return pl.pallas_call(
        zone_kernel,
        out_shape=jax.ShapeDtypeStruct((owned, panel, modes), jnp.float32),
        in_specs=[
            pl.BlockSpec(memory_space=pltpu.SMEM),
            pl.BlockSpec(memory_space=pltpu.SMEM),
            pl.BlockSpec(memory_space=pltpu.VMEM),
            pl.BlockSpec(memory_space=pltpu.VMEM),
        ],
        out_specs=pl.BlockSpec(memory_space=pltpu.VMEM),
    )(me.reshape(1), source, arrived, scale)


def solution(mesh):
    placed = (P("mode", "tile", None), P("tile", None), P("tile", None), P())
    return jax.shard_map(
        per_device, mesh=mesh, in_specs=placed, out_specs=P("tile", "mode", None), check_vma=False
    )
```

```python
import functools

import jax
import jax.numpy as jnp
from jax import lax
from jax.experimental import pallas as pl
from jax.experimental.pallas import tpu as pltpu
from jax.sharding import PartitionSpec as P

ZONES = 512
POISSON = 0.3
SHEAR = 2.0 * (1.0 - POISSON)
LANES = 128


def bend_row(up, mid, down, first_col, last_col):
    up = up.astype(jnp.float32)
    mid = mid.astype(jnp.float32)
    down = down.astype(jnp.float32)
    width = mid.shape[1]

    def before(cells):
        return jnp.where(first_col, 0.0, pltpu.roll(cells, 1, 1))

    def after(cells):
        return jnp.where(last_col, 0.0, pltpu.roll(cells, width - 1, 1))

    along_x = down - 2.0 * mid + up
    along_y = after(mid) - 2.0 * mid + before(mid)
    slope = down - up
    twist = 0.25 * (after(slope) - before(slope))
    return [c.astype(jnp.bfloat16) for c in (along_x, along_y, twist)]


def pair_kernel(
    sizes, own_ref, stiff_ref, slot_ref, out_ref, total_ref,
    frames, half_frame, left_s, right_s, acc, sums, results, returned, arrived, tile_sums, mode_sums,
    halo_send, halo_recv, row_send, row_recv, back_send, back_recv, block_send, block_recv,
    tsum_send, tsum_recv, msum_send, msum_recv,
):
    tiles, panels, entries = sizes
    rows, panel, width = own_ref.shape
    half = panels // 2
    part = half_frame.shape[2]
    shift = width - part
    tall, wide = tiles * panel, entries * panel
    tile = lax.axis_index("tile")
    me = lax.axis_index("mode")

    def tile_peer(step):
        return lax.rem(tile + step, tiles)

    def mode_peer(step):
        return lax.rem(me + step, panels)

    def to(src, dst, send, recv, at_tile, at_mode):
        return pltpu.make_async_remote_copy(
            src_ref=src, dst_ref=dst, send_sem=send, recv_sem=recv,
            device_id=(at_tile, at_mode), device_id_type=pl.DeviceIdType.MESH,
        )

    barrier = pltpu.get_barrier_semaphore()
    for step in range(1, panels):
        pl.semaphore_signal(barrier, inc=1, device_id=(tile, mode_peer(step)), device_id_type=pl.DeviceIdType.MESH)

    def greet(step, carry):
        pl.semaphore_signal(barrier, inc=1, device_id=(tile_peer(step), me), device_id_type=pl.DeviceIdType.MESH)
        return carry

    lax.fori_loop(1, tiles, greet, 0)

    def greet_far(step, carry):
        pl.semaphore_signal(
            barrier, inc=1, device_id=(tile_peer(step), mode_peer(half)), device_id_type=pl.DeviceIdType.MESH
        )
        return carry

    lax.fori_loop(1, tiles, greet_far, 0)

    first_tile, last_tile = tile == 0, tile == tiles - 1

    @pl.when(first_tile)
    def _():
        for d in range(half):
            frames[d, 0] = jnp.zeros((panel, width), jnp.bfloat16)
        half_frame[0] = jnp.zeros((panel, part), jnp.bfloat16)

    @pl.when(last_tile)
    def _():
        for d in range(half):
            frames[d, rows + 1] = jnp.zeros((panel, width), jnp.bfloat16)
        half_frame[rows + 1] = jnp.zeros((panel, part), jnp.bfloat16)

    pl.semaphore_wait(barrier, panels - 1 + 2 * (tiles - 1))

    their_start = pl.multiple_of(jnp.where(me < half, shift, 0), LANES)
    mine_start = pl.multiple_of(jnp.where(me < half, 0, shift), LANES)

    def row_copy(d, row):
        if d == half:
            src, dst = own_ref.at[row, :, pl.ds(their_start, part)], half_frame.at[row + 1]
        else:
            src, dst = own_ref.at[row], frames.at[d, row + 1]
        return to(src, dst, row_send.at[d, row], row_recv.at[d, row], tile, mode_peer(panels - d))

    def edge_copies(d):
        frame = half_frame if d == half else frames.at[d]
        top = own_ref.at[0] if d == 0 else frame.at[1]
        bottom = own_ref.at[rows - 1] if d == 0 else frame.at[rows]
        upward = to(top, frame.at[rows + 1], halo_send.at[d, 0], halo_recv.at[d, 0], jnp.maximum(tile - 1, 0), me)
        downward = to(
            bottom, frame.at[0], halo_send.at[d, 1], halo_recv.at[d, 1], jnp.minimum(tile + 1, tiles - 1), me
        )
        return upward, downward

    def start_edges(d):
        upward, downward = edge_copies(d)
        pl.when(jnp.logical_not(first_tile))(upward.start)
        pl.when(jnp.logical_not(last_tile))(downward.start)

    def await_edges(d):
        upward, downward = edge_copies(d)
        pl.when(jnp.logical_not(last_tile))(upward.wait_recv)
        pl.when(jnp.logical_not(first_tile))(downward.wait_recv)

    def finish_edges(d):
        upward, downward = edge_copies(d)
        pl.when(jnp.logical_not(first_tile))(upward.wait_send)
        pl.when(jnp.logical_not(last_tile))(downward.wait_send)

    start_edges(0)
    for d in range(1, half + 1):
        row_copy(d, 0).start()
        row_copy(d, rows - 1).start()
    for d in range(1, half + 1):
        for row in range(1, rows - 1):
            row_copy(d, row).start()
    for row in range(rows):
        frames[0, row + 1] = own_ref[row]

    sums[...] = jnp.zeros_like(sums)

    def block_copy(block, step):
        peer = tile_peer(step)
        return to(
            results.at[block, peer], arrived.at[block, tile],
            block_send.at[block, step], block_recv.at[block, step], peer, me,
        )

    def start_blocks(block):
        def go(step, carry):
            block_copy(block, step).start()
            return carry

        lax.fori_loop(1, tiles, go, 0)
        arrived[block, tile] = results[block, tile]

    def back_copy(d):
        block = results.at[panels + d]
        return to(block, returned.at[d], back_send.at[d], back_recv.at[d], tile, mode_peer(d))

    def far_copy(step):
        peer = tile_peer(step)
        return to(
            results.at[panels + half, peer], arrived.at[panels, tile],
            block_send.at[panels, step], block_recv.at[panels, step], peer, mode_peer(half),
        )

    def msum_copy(step):
        return to(
            mode_sums.at[me], mode_sums.at[me], msum_send.at[step], msum_recv.at[step], tile, mode_peer(step)
        )

    def pass_on():
        def take_sum(step, carry):
            tsum_copy(step).wait()
            return carry

        lax.fori_loop(1, tiles, take_sum, 0)
        mode_sums[me] = jnp.sum(tile_sums[...], axis=0)
        for step in range(1, panels):
            msum_copy(step).start()
        for e in range(1, half):
            back_copy(e).wait()
            results[panels - e] = returned[e]
            start_blocks(panels - e)

    def tsum_copy(step):
        return to(sums, tile_sums.at[tile], tsum_send.at[step], tsum_recv.at[step], tile_peer(step), me)

    def keep(block, values):
        results[block] = values.reshape(tiles, panel, wide)

    for d in range(1, half + 1):
        split = d == half
        span = part if split else width
        column = lax.broadcasted_iota(jnp.int32, (panel, span), 1)
        first_col, last_col = column == 0, column == span - 1
        if split:
            inside = jnp.where(me < half, (column < width // 2).astype(jnp.int32), (column >= LANES).astype(jnp.int32))
        row_copy(d, 0).wait_recv()
        row_copy(d, rows - 1).wait_recv()
        start_edges(d)
        row_copy(d, 1).wait_recv()
        acc[...] = jnp.zeros_like(acc)

        def one_row(k, carry):
            row = lax.rem(k + 1, rows)

            @pl.when(k < rows - 3)
            def _():
                row_copy(d, k + 2).wait_recv()

            @pl.when(k == rows - 2)
            def _():
                if d == 1:
                    await_edges(0)
                await_edges(d)
                if split:
                    pass_on()

            if split:
                here = pl.ds(mine_start, part)
                stiff, slot = stiff_ref[row, :, here], slot_ref[row, :, here]
                mine = [frames[0, row + i, :, here] for i in range(3)]
                theirs = [half_frame[row + i] for i in range(3)]
            else:
                stiff, slot = stiff_ref[row], slot_ref[row]
                mine = [frames[0, row + i] for i in range(3)]
                theirs = [frames[d, row + i] for i in range(3)]
            owner = slot // entries
            entry = slot - owner * entries
            owner_b = jnp.broadcast_to(owner, (panel, span))
            entry_b = jnp.broadcast_to(entry, (panel, span))
            if split:
                owner_b = jnp.where(inside == 1, owner_b, tiles)
            lefts, rights = [], []
            for number, taken in enumerate((mine, theirs)):
                bend = bend_row(*taken, first_col, last_col)
                bx, by, bt = [c.astype(jnp.float32) for c in bend]
                lx = stiff * (bx + POISSON * by)
                ly = stiff * (by + POISSON * bx)
                lt = stiff * (SHEAR * bt)
                if number == 0 and d == 1:
                    row_sum = jnp.sum(lx * bx + ly * by + lt * bt, axis=1, keepdims=True)
                    sums[...] += jnp.broadcast_to(row_sum, sums.shape)
                rights.append(bend)
                lefts.append([c.astype(jnp.bfloat16) for c in (lx, ly, lt)])
            for k in range(tiles):
                mask = (owner_b == k).astype(jnp.float32).astype(jnp.bfloat16)
                for c in range(3):
                    for n in range(2):
                        left_s[c, pl.ds((n * tiles + k) * panel, panel), pl.ds(0, span)] = lefts[n][c] * mask
            for k in range(entries):
                mask = (entry_b == k).astype(jnp.float32).astype(jnp.bfloat16)
                for c in range(3):
                    for n in range(2):
                        right_s[c, pl.ds((n * entries + k) * panel, panel), pl.ds(0, span)] = rights[n][c] * mask
            for c in range(3):
                acc[...] += lax.dot_general(
                    left_s[c, :, pl.ds(0, span)], right_s[c, :, pl.ds(0, span)],
                    (((1,), (1,)), ((), ())), preferred_element_type=jnp.float32,
                )
            return carry

        lax.fori_loop(0, rows, one_row, 0)
        keep(panels + d, acc[pl.ds(tall, tall), pl.ds(0, wide)])
        if split:

            def send_far(step, carry):
                far_copy(step).start()
                return carry

            lax.fori_loop(0, tiles, send_far, 0)
        else:
            back_copy(d).start()
        keep(d, acc[pl.ds(0, tall), pl.ds(wide, wide)])
        start_blocks(d)
        if d == 1:

            def send_sum(step, carry):
                tsum_copy(step).start()
                return carry

            lax.fori_loop(1, tiles, send_sum, 0)
            tile_sums[tile] = sums[...]
            keep(0, acc[pl.ds(0, tall), pl.ds(0, wide)])
            start_blocks(0)

    for d in range(half + 1):
        finish_edges(d)
    for d in range(1, half + 1):
        for row in range(rows):
            row_copy(d, row).wait_send()
    for step in range(1, panels):
        msum_copy(step).wait()

    for block in range(panels):
        def take(step, carry):
            block_copy(block, step).wait()
            return carry

        lax.fori_loop(1, tiles, take, 0)

    def take_far(step, carry):
        far_copy(step).wait()
        return carry

    lax.fori_loop(0, tiles, take_far, 0)
    for block in range(panels):
        out_ref[block] = arrived[block]
    out_ref[half] += arrived[panels]
    total_ref[...] = mode_sums[...]


def pair_sums(own, stiff, slot, tiles, panels, entries):
    rows, panel, width = own.shape
    half = panels // 2
    part = width // 2 + LANES
    tall, wide = 2 * tiles * panel, 2 * entries * panel
    whole = pl.BlockSpec(memory_space=pltpu.VMEM)
    blocks = (panels, tiles, panel, entries * panel)
    dma = pltpu.SemaphoreType.DMA
    f32, bf16 = jnp.float32, jnp.bfloat16
    return pl.pallas_call(
        functools.partial(pair_kernel, (tiles, panels, entries)),
        out_shape=(
            jax.ShapeDtypeStruct(blocks, f32),
            jax.ShapeDtypeStruct((panels, panel, LANES), f32),
        ),
        in_specs=[whole] * 3,
        out_specs=(whole, whole),
        scratch_shapes=[
            pltpu.VMEM((half, rows + 2, panel, width), bf16),
            pltpu.VMEM((rows + 2, panel, part), bf16),
            pltpu.VMEM((3, tall, width), bf16),
            pltpu.VMEM((3, wide, width), bf16),
            pltpu.VMEM((tall, wide), f32),
            pltpu.VMEM((panel, LANES), f32),
            pltpu.VMEM((panels + half + 1,) + blocks[1:], f32),
            pltpu.VMEM((half,) + blocks[1:], f32),
            pltpu.VMEM((panels + 1,) + blocks[1:], f32),
            pltpu.VMEM((tiles, panel, LANES), f32),
            pltpu.VMEM((panels, panel, LANES), f32),
            dma((half + 1, 2)), dma((half + 1, 2)),
            dma((half + 1, rows)), dma((half + 1, rows)),
            dma((half,)), dma((half,)),
            dma((panels + 1, tiles)), dma((panels + 1, tiles)),
            dma((tiles,)), dma((tiles,)),
            dma((panels,)), dma((panels,)),
        ],
        compiler_params=pltpu.CompilerParams(
            vmem_limit_bytes=48 << 20, collective_id=0, has_side_effects=True
        ),
        cost_estimate=pl.CostEstimate(
            flops=6 * tall * wide * rows * width * half, bytes_accessed=2 * own.size * 2, transcendentals=0
        ),
    )(own, stiff.reshape(rows, 1, width), slot.reshape(rows, 1, width))


def zone_kernel(place_ref, source_ref, blocks_ref, sums_ref, out_ref):
    panels, tiles, panel, _ = blocks_ref.shape
    entries = source_ref.shape[2]
    tile, me = place_ref[0], place_ref[1]
    out_ref[...] = jnp.zeros_like(out_ref)
    shape = (panel, panel)
    diagonal = lax.broadcasted_iota(jnp.int32, shape, 0) == lax.broadcasted_iota(jnp.int32, shape, 1)
    across = jnp.concatenate(
        [
            jnp.sum(jnp.where(diagonal, sums_ref[g][:, :panel], 0.0), axis=0, keepdims=True)
            for g in range(panels)
        ],
        axis=1,
    )
    scale = (0.5 * ZONES) / jnp.sqrt((0.5 * sums_ref[me][:, :1]) * (0.5 * across))

    def one_tile(source, carry):
        got = [blocks_ref[lax.rem(g - me + panels, panels), source] for g in range(panels)]
        for k in range(entries):
            row = jnp.concatenate([b[:, k * panel : (k + 1) * panel] for b in got], axis=1)
            zone = source_ref[source, tile, k]
            out_ref[zone] += row * scale
        return carry

    lax.fori_loop(0, tiles, one_tile, 0)


def per_device(mode_shapes, stiffness, node_slot, slot_zone):
    panel = mode_shapes.shape[0]
    tiles = lax.axis_size("tile")
    panels = lax.axis_size("mode")
    modes = panel * panels
    entries = slot_zone.shape[2]
    owned = ZONES // tiles
    place = jnp.stack([lax.axis_index("tile"), lax.axis_index("mode")]).astype(jnp.int32)

    own = mode_shapes.transpose(1, 0, 2)
    arrived, sums = pair_sums(own, stiffness, node_slot, tiles, panels, entries)
    return pl.pallas_call(
        zone_kernel,
        out_shape=jax.ShapeDtypeStruct((owned, panel, modes), jnp.float32),
        in_specs=[
            pl.BlockSpec(memory_space=pltpu.SMEM),
            pl.BlockSpec(memory_space=pltpu.SMEM),
            pl.BlockSpec(memory_space=pltpu.VMEM),
            pl.BlockSpec(memory_space=pltpu.VMEM),
        ],
        out_specs=pl.BlockSpec(memory_space=pltpu.VMEM),
    )(place, slot_zone, arrived, sums)


def solution(mesh):
    placed = (P("mode", "tile", None), P("tile", None), P("tile", None), P())
    return jax.shard_map(
        per_device, mesh=mesh, in_specs=placed, out_specs=P("tile", "mode", None), check_vma=False
    )
```

```python
import functools

import jax
import jax.numpy as jnp
from jax import lax
from jax.experimental import pallas as pl
from jax.experimental.pallas import tpu as pltpu
from jax.sharding import PartitionSpec as P

ZONES = 512
POISSON = 0.3
SHEAR = 2.0 * (1.0 - POISSON)
LANES = 128


def bend_row(up, mid, down, first_col, last_col):
    up = up.astype(jnp.float32)
    mid = mid.astype(jnp.float32)
    down = down.astype(jnp.float32)
    width = mid.shape[1]

    def before(cells):
        return jnp.where(first_col, 0.0, pltpu.roll(cells, 1, 1))

    def after(cells):
        return jnp.where(last_col, 0.0, pltpu.roll(cells, width - 1, 1))

    along_x = down - 2.0 * mid + up
    along_y = after(mid) - 2.0 * mid + before(mid)
    slope = down - up
    twist = 0.25 * (after(slope) - before(slope))
    return [c.astype(jnp.bfloat16) for c in (along_x, along_y, twist)]


def pair_kernel(
    sizes, own_ref, stiff_ref, slot_ref, out_ref, total_ref,
    frames, half_frame, left_s, right_s, acc, sums, results, returned, arrived, tile_sums, mode_sums,
    halo_send, halo_recv, row_send, row_recv, back_send, back_recv, block_send, block_recv,
    tsum_send, tsum_recv, msum_send, msum_recv,
):
    tiles, panels, entries = sizes
    rows, panel, width = own_ref.shape
    half = panels // 2
    part = half_frame.shape[2]
    shift = width - part
    tall, wide = tiles * panel, entries * panel
    tile = lax.axis_index("tile")
    me = lax.axis_index("mode")

    def tile_peer(step):
        return lax.rem(tile + step, tiles)

    def mode_peer(step):
        return lax.rem(me + step, panels)

    def to(src, dst, send, recv, at_tile, at_mode):
        return pltpu.make_async_remote_copy(
            src_ref=src, dst_ref=dst, send_sem=send, recv_sem=recv,
            device_id=(at_tile, at_mode), device_id_type=pl.DeviceIdType.MESH,
        )

    barrier = pltpu.get_barrier_semaphore()
    for step in range(1, panels):
        pl.semaphore_signal(barrier, inc=1, device_id=(tile, mode_peer(step)), device_id_type=pl.DeviceIdType.MESH)

    def greet(step, carry):
        pl.semaphore_signal(barrier, inc=1, device_id=(tile_peer(step), me), device_id_type=pl.DeviceIdType.MESH)
        return carry

    lax.fori_loop(1, tiles, greet, 0)

    def greet_far(step, carry):
        pl.semaphore_signal(
            barrier, inc=1, device_id=(tile_peer(step), mode_peer(half)), device_id_type=pl.DeviceIdType.MESH
        )
        return carry

    lax.fori_loop(1, tiles, greet_far, 0)

    first_tile, last_tile = tile == 0, tile == tiles - 1

    @pl.when(first_tile)
    def _():
        for d in range(half):
            frames[d, 0] = jnp.zeros((panel, width), jnp.bfloat16)
        half_frame[0] = jnp.zeros((panel, part), jnp.bfloat16)

    @pl.when(last_tile)
    def _():
        for d in range(half):
            frames[d, rows + 1] = jnp.zeros((panel, width), jnp.bfloat16)
        half_frame[rows + 1] = jnp.zeros((panel, part), jnp.bfloat16)

    pl.semaphore_wait(barrier, panels - 1 + 2 * (tiles - 1))

    their_start = pl.multiple_of(jnp.where(me < half, shift, 0), LANES)
    mine_start = pl.multiple_of(jnp.where(me < half, 0, shift), LANES)

    def row_copy(d, row):
        if d == half:
            src, dst = own_ref.at[row, :, pl.ds(their_start, part)], half_frame.at[row + 1]
        else:
            src, dst = own_ref.at[row], frames.at[d, row + 1]
        return to(src, dst, row_send.at[d, row], row_recv.at[d, row], tile, mode_peer(panels - d))

    def edge_copies(d):
        frame = half_frame if d == half else frames.at[d]
        top = own_ref.at[0] if d == 0 else frame.at[1]
        bottom = own_ref.at[rows - 1] if d == 0 else frame.at[rows]
        upward = to(top, frame.at[rows + 1], halo_send.at[d, 0], halo_recv.at[d, 0], jnp.maximum(tile - 1, 0), me)
        downward = to(
            bottom, frame.at[0], halo_send.at[d, 1], halo_recv.at[d, 1], jnp.minimum(tile + 1, tiles - 1), me
        )
        return upward, downward

    def start_edges(d):
        upward, downward = edge_copies(d)
        pl.when(jnp.logical_not(first_tile))(upward.start)
        pl.when(jnp.logical_not(last_tile))(downward.start)

    def await_edges(d):
        upward, downward = edge_copies(d)
        pl.when(jnp.logical_not(last_tile))(upward.wait_recv)
        pl.when(jnp.logical_not(first_tile))(downward.wait_recv)

    def finish_edges(d):
        upward, downward = edge_copies(d)
        pl.when(jnp.logical_not(first_tile))(upward.wait_send)
        pl.when(jnp.logical_not(last_tile))(downward.wait_send)

    start_edges(0)
    for d in range(1, half + 1):
        for row in (0, rows - 1, *range(1, rows - 1)):
            row_copy(d, row).start()
    for row in range(rows):
        frames[0, row + 1] = own_ref[row]

    sums[...] = jnp.zeros_like(sums)

    def block_copy(block, step):
        peer = tile_peer(step)
        return to(
            results.at[block, peer], arrived.at[block, tile],
            block_send.at[block, step], block_recv.at[block, step], peer, me,
        )

    def start_blocks(block):
        def go(step, carry):
            block_copy(block, step).start()
            return carry

        lax.fori_loop(1, tiles, go, 0)
        arrived[block, tile] = results[block, tile]

    def back_copy(d):
        block = results.at[panels + d]
        return to(block, returned.at[d], back_send.at[d], back_recv.at[d], tile, mode_peer(d))

    def far_copy(step):
        peer = tile_peer(step)
        return to(
            results.at[panels + half, peer], arrived.at[panels, tile],
            block_send.at[panels, step], block_recv.at[panels, step], peer, mode_peer(half),
        )

    def msum_copy(step):
        return to(
            mode_sums.at[me], mode_sums.at[me], msum_send.at[step], msum_recv.at[step], tile, mode_peer(step)
        )

    def pass_on():
        def take_sum(step, carry):
            tsum_copy(step).wait()
            return carry

        lax.fori_loop(1, tiles, take_sum, 0)
        mode_sums[me] = jnp.sum(tile_sums[...], axis=0)
        for step in range(1, panels):
            msum_copy(step).start()
        for e in range(1, half):
            back_copy(e).wait()
            results[panels - e] = returned[e]
            start_blocks(panels - e)

    def tsum_copy(step):
        return to(sums, tile_sums.at[tile], tsum_send.at[step], tsum_recv.at[step], tile_peer(step), me)

    def keep(block, values):
        results[block] = values.reshape(tiles, panel, wide)

    for d in range(1, half + 1):
        split = d == half
        span = part if split else width
        column = lax.broadcasted_iota(jnp.int32, (panel, span), 1)
        first_col, last_col = column == 0, column == span - 1
        if split:
            inside = jnp.where(me < half, (column < width // 2).astype(jnp.int32), (column >= LANES).astype(jnp.int32))
        row_copy(d, 0).wait_recv()
        row_copy(d, rows - 1).wait_recv()
        start_edges(d)
        row_copy(d, 1).wait_recv()
        acc[...] = jnp.zeros_like(acc)

        def one_row(k, carry):
            row = lax.rem(k + 1, rows)

            @pl.when(k < rows - 3)
            def _():
                row_copy(d, k + 2).wait_recv()

            @pl.when(k == rows - 2)
            def _():
                if d == 1:
                    await_edges(0)
                await_edges(d)
                if split:
                    pass_on()

            if split:
                here = pl.ds(mine_start, part)
                stiff, slot = stiff_ref[row, :, here], slot_ref[row, :, here]
                mine = [frames[0, row + i, :, here] for i in range(3)]
                theirs = [half_frame[row + i] for i in range(3)]
            else:
                stiff, slot = stiff_ref[row], slot_ref[row]
                mine = [frames[0, row + i] for i in range(3)]
                theirs = [frames[d, row + i] for i in range(3)]
            owner = slot // entries
            entry = slot - owner * entries
            owner_b = jnp.broadcast_to(owner, (panel, span))
            entry_b = jnp.broadcast_to(entry, (panel, span))
            if split:
                owner_b = jnp.where(inside == 1, owner_b, tiles)
            lefts, rights = [], []
            for number, taken in enumerate((mine, theirs)):
                bend = bend_row(*taken, first_col, last_col)
                bx, by, bt = [c.astype(jnp.float32) for c in bend]
                lx = stiff * (bx + POISSON * by)
                ly = stiff * (by + POISSON * bx)
                lt = stiff * (SHEAR * bt)
                if number == 0 and d == 1:
                    row_sum = jnp.sum(lx * bx + ly * by + lt * bt, axis=1, keepdims=True)
                    sums[...] += jnp.broadcast_to(row_sum, sums.shape)
                rights.append(bend)
                lefts.append([c.astype(jnp.bfloat16) for c in (lx, ly, lt)])
            for k in range(tiles):
                mask = (owner_b == k).astype(jnp.float32).astype(jnp.bfloat16)
                for c in range(3):
                    for n in range(2):
                        left_s[c, pl.ds((n * tiles + k) * panel, panel), pl.ds(0, span)] = lefts[n][c] * mask
            for k in range(entries):
                mask = (entry_b == k).astype(jnp.float32).astype(jnp.bfloat16)
                for c in range(3):
                    for n in range(2):
                        right_s[c, pl.ds((n * entries + k) * panel, panel), pl.ds(0, span)] = rights[n][c] * mask
            for c in range(3):
                acc[...] += lax.dot_general(
                    left_s[c, :, pl.ds(0, span)], right_s[c, :, pl.ds(0, span)],
                    (((1,), (1,)), ((), ())), preferred_element_type=jnp.float32,
                )
            return carry

        lax.fori_loop(0, rows, one_row, 0)
        keep(panels + d, acc[pl.ds(tall, tall), pl.ds(0, wide)])
        if split:

            def send_far(step, carry):
                far_copy(step).start()
                return carry

            lax.fori_loop(0, tiles, send_far, 0)
        else:
            back_copy(d).start()
        keep(d, acc[pl.ds(0, tall), pl.ds(wide, wide)])
        start_blocks(d)
        if d == 1:

            def send_sum(step, carry):
                tsum_copy(step).start()
                return carry

            lax.fori_loop(1, tiles, send_sum, 0)
            tile_sums[tile] = sums[...]
            keep(0, acc[pl.ds(0, tall), pl.ds(0, wide)])
            start_blocks(0)

    for d in range(half + 1):
        finish_edges(d)
    for d in range(1, half + 1):
        for row in range(rows):
            row_copy(d, row).wait_send()
    for step in range(1, panels):
        msum_copy(step).wait()

    for block in range(panels):
        def take(step, carry):
            block_copy(block, step).wait()
            return carry

        lax.fori_loop(1, tiles, take, 0)

    def take_far(step, carry):
        far_copy(step).wait()
        return carry

    lax.fori_loop(0, tiles, take_far, 0)
    for block in range(panels):
        out_ref[block] = arrived[block]
    out_ref[half] += arrived[panels]
    total_ref[...] = mode_sums[...]


def pair_sums(own, stiff, slot, tiles, panels, entries):
    rows, panel, width = own.shape
    half = panels // 2
    part = width // 2 + LANES
    tall, wide = 2 * tiles * panel, 2 * entries * panel
    whole = pl.BlockSpec(memory_space=pltpu.VMEM)
    blocks = (panels, tiles, panel, entries * panel)
    dma = pltpu.SemaphoreType.DMA
    f32, bf16 = jnp.float32, jnp.bfloat16
    return pl.pallas_call(
        functools.partial(pair_kernel, (tiles, panels, entries)),
        out_shape=(
            jax.ShapeDtypeStruct(blocks, f32),
            jax.ShapeDtypeStruct((panels, panel, LANES), f32),
        ),
        in_specs=[whole] * 3,
        out_specs=(whole, whole),
        scratch_shapes=[
            pltpu.VMEM((half, rows + 2, panel, width), bf16),
            pltpu.VMEM((rows + 2, panel, part), bf16),
            pltpu.VMEM((3, tall, width), bf16),
            pltpu.VMEM((3, wide, width), bf16),
            pltpu.VMEM((tall, wide), f32),
            pltpu.VMEM((panel, LANES), f32),
            pltpu.VMEM((panels + half + 1,) + blocks[1:], f32),
            pltpu.VMEM((half,) + blocks[1:], f32),
            pltpu.VMEM((panels + 1,) + blocks[1:], f32),
            pltpu.VMEM((tiles, panel, LANES), f32),
            pltpu.VMEM((panels, panel, LANES), f32),
            dma((half + 1, 2)), dma((half + 1, 2)),
            dma((half + 1, rows)), dma((half + 1, rows)),
            dma((half,)), dma((half,)),
            dma((panels + 1, tiles)), dma((panels + 1, tiles)),
            dma((tiles,)), dma((tiles,)),
            dma((panels,)), dma((panels,)),
        ],
        compiler_params=pltpu.CompilerParams(
            vmem_limit_bytes=48 << 20, collective_id=0, has_side_effects=True
        ),
        cost_estimate=pl.CostEstimate(
            flops=6 * tall * wide * rows * width * half, bytes_accessed=2 * own.size * 2, transcendentals=0
        ),
    )(own, stiff.reshape(rows, 1, width), slot.reshape(rows, 1, width))


def zone_kernel(source_ref, blocks_ref, sums_ref, out_ref):
    panels, tiles, panel, _ = blocks_ref.shape
    entries = source_ref.shape[2]
    tile, me = lax.axis_index("tile"), lax.axis_index("mode")
    out_ref[...] = jnp.zeros_like(out_ref)
    shape = (panel, panel)
    diagonal = lax.broadcasted_iota(jnp.int32, shape, 0) == lax.broadcasted_iota(jnp.int32, shape, 1)
    across = jnp.concatenate(
        [
            jnp.sum(jnp.where(diagonal, sums_ref[g][:, :panel], 0.0), axis=0, keepdims=True)
            for g in range(panels)
        ],
        axis=1,
    )
    scale = (0.5 * ZONES) / jnp.sqrt((0.5 * sums_ref[me][:, :1]) * (0.5 * across))

    def one_tile(source, carry):
        got = [blocks_ref[lax.rem(g - me + panels, panels), source] for g in range(panels)]
        for k in range(entries):
            row = jnp.concatenate([b[:, k * panel : (k + 1) * panel] for b in got], axis=1)
            zone = source_ref[source, tile, k]
            out_ref[zone] += row * scale
        return carry

    lax.fori_loop(0, tiles, one_tile, 0)


def per_device(mode_shapes, stiffness, node_slot, slot_zone):
    panel = mode_shapes.shape[0]
    tiles = lax.axis_size("tile")
    panels = lax.axis_size("mode")
    modes = panel * panels
    entries = slot_zone.shape[2]
    owned = ZONES // tiles

    own = mode_shapes.transpose(1, 0, 2)
    arrived, sums = pair_sums(own, stiffness, node_slot, tiles, panels, entries)
    return pl.pallas_call(
        zone_kernel,
        out_shape=jax.ShapeDtypeStruct((owned, panel, modes), jnp.float32),
        in_specs=[
            pl.BlockSpec(memory_space=pltpu.SMEM),
            pl.BlockSpec(memory_space=pltpu.VMEM),
            pl.BlockSpec(memory_space=pltpu.VMEM),
        ],
        out_specs=pl.BlockSpec(memory_space=pltpu.VMEM),
    )(slot_zone, arrived, sums)


def solution(mesh):
    placed = (P("mode", "tile", None), P("tile", None), P("tile", None), P())
    return jax.shard_map(
        per_device, mesh=mesh, in_specs=placed, out_specs=P("tile", "mode", None), check_vma=False
    )
```
